256 devices in a mesh: row: 128 (over x, y, z), band: 2 (over core).
Axes of the slice: x: 4, y: 4, z: 8, core: 2. Of those that a mesh axis runs over, the one named last changes fastest.
Arguments:
- hamiltonian: bfloat16 [1280, 32, 128, 128], P('row'), may hold values from -0.09375 to 0.09375
- neighbours: int32 [1280, 32], P('row'), may hold values from 0 to 1279, as said below
- counts: int32 [1280], P('row'), may hold values from 16 to 32
- vectors: bfloat16 [163840, 128], P('row', 'band'), may hold values from -6 to 6
Outputs:
- filtered: bfloat16 [163840, 128], P('row', 'band')
- gram: float32 [128, 128], P('band')
- projected: float32 [128, 128], P('band')
The draws below stay inside these ranges and needn't reach their ends.
Inputs may be any that keep to these rules, and one draw needn't show every extreme that they name: `neighbours`: entry [r, 0] is r; every entry lies within 8 of its block row r.
All inputs are finite; a program needn't handle non-finite values.
Results may differ from the reference program's by a relative error of at most 0.022.
Values may be sent and summed in bfloat16 or wider, within the bound.
No kernel may reach another device: no remote copies, remote signals or barrier semaphores. Data moves between devices by JAX's collectives and lax.ppermute only.
A program may use at most 128 MiB of HBM per device.

```python
import jax
import jax.numpy as jnp
from jax import lax

B = 128
M = 128
NNZ_MAX = 32
DIST = 8
NB = 1280
ROWS = 163840


def draw_neighbours(key, part):
    key = jax.random.fold_in(key, 11)
    offsets = jax.random.randint(key, (NB, NNZ_MAX), -DIST, DIST + 1)
    column = jnp.arange(NNZ_MAX, dtype=jnp.int32)[None, :]
    offsets = jnp.where(column == 0, 0, offsets)
    rowids = jnp.arange(NB, dtype=jnp.int32)[:, None]
    return jnp.clip(rowids + offsets, 0, NB - 1).astype(jnp.int32)


def draw_counts(key, part):
    key = jax.random.fold_in(key, 23)
    drawn = jax.random.randint(key, (NB,), NNZ_MAX // 2, NNZ_MAX + 1)
    rowids = jnp.arange(NB, dtype=jnp.int32)
    return jnp.where(rowids == 0, NNZ_MAX, drawn).astype(jnp.int32)


def level_of(stream_key, shape, shards, least, top_value):
    factor_of, own = 1.0, jax.random.fold_in(stream_key, 6)
    for position, parts in shards:
        steps = jnp.exp(jax.random.uniform(jax.random.fold_in(own, position), (parts,), jnp.float32, least / len(shards), top_value / len(shards)))
        factor_of = factor_of * jnp.repeat(steps, shape[position] // parts).reshape([-1 if axis == position else 1 for axis in range(len(shape))])
    return factor_of


def scatter_about(rng, shape, scale, bound, split=(), kind=jnp.bfloat16):
    gain = level_of(rng, shape, split, -0.22, 0.18) if split else 1.0
    entries = jax.random.normal(rng, shape, jnp.float32) * scale * gain
    return jnp.minimum(jnp.maximum(entries, -bound), bound).astype(kind)


def setup_inputs(seed: int = 0) -> dict:
    arg_keys = jax.random.split(jax.random.key(seed), 5)
    hamiltonian = scatter_about(arg_keys[0], (NB, NNZ_MAX, B, B), (B * NNZ_MAX) ** -0.5, 0.09375, ((0, 128),))
    neighbours = draw_neighbours(jax.random.fold_in(arg_keys[4], 71), 0)
    counts = draw_counts(jax.random.fold_in(arg_keys[4], 71), 0)
    vectors = scatter_about(arg_keys[3], (ROWS, M), 1.0, 6.0, ((0, 128), (1, 2)))
    return dict(hamiltonian=hamiltonian, neighbours=neighbours, counts=counts, vectors=vectors)


def apply_blocks(hamiltonian, neighbours, counts, field):
    blocks = field.reshape(NB, B, field.shape[1])
    slots = jnp.arange(NNZ_MAX, dtype=jnp.int32)
    groups = NB // 16

    def one_group(item):
        block_rows, neighbour_rows, count_rows = item
        live = (slots[None, :] < count_rows[:, None]).astype(jnp.float32)
        taken = blocks[neighbour_rows].astype(jnp.float32) * live[:, :, None, None]
        return jnp.einsum("gsij,gsjm->gim", block_rows.astype(jnp.float32), taken)

    result = lax.map(one_group, (hamiltonian.reshape(groups, 16, NNZ_MAX, B, B),
                                 neighbours.reshape(groups, 16, NNZ_MAX),
                                 counts.reshape(groups, 16)))
    return result.reshape(NB * B, field.shape[1])


def reference(hamiltonian, neighbours, counts, vectors):
    level1 = apply_blocks(hamiltonian, neighbours, counts, vectors).astype(jnp.bfloat16)
    older, newer = vectors, level1
    for degree in range(3):
        applied = apply_blocks(hamiltonian, neighbours, counts, newer)
        nextone = (2.0 * applied - older.astype(jnp.float32)).astype(jnp.bfloat16)
        older, newer = newer, nextone
    filtered = newer
    image = apply_blocks(hamiltonian, neighbours, counts, filtered).astype(jnp.bfloat16)
    scale_rows = 1.0 / (NB * B)
    gram = jnp.dot(filtered.T, filtered, preferred_element_type=jnp.float32) * scale_rows
    projected = jnp.dot(filtered.T, image, preferred_element_type=jnp.float32) * scale_rows
    return filtered, gram, projected
```

```python
import jax
import jax.numpy as jnp
from jax import lax
from jax.experimental import pallas as pl
from jax.experimental.pallas import tpu as pltpu
from jax.sharding import Mesh, PartitionSpec as P

B = 128
DIST = 8
ROWS = ("x", "y", "z")
SURE = 16
CHUNK = 4
NT = (((1,), (1,)), ((), ()))
MIB = 1024 * 1024


def dot_nt(a, b):
    return lax.dot_general(a, b, NT, preferred_element_type=jnp.float32)


def slot_order(neighbours, counts, first_block):
    slot_count = neighbours.shape[1]
    slots = jnp.arange(slot_count, dtype=jnp.int32)[None, :]
    column = neighbours - first_block + DIST
    dead = neighbours.shape[0] + 2 * DIST
    key = jnp.where(slots < counts[:, None], column, dead) * slot_count + slots
    rank = jnp.sum((key[:, None, :] < key[:, :, None]).astype(jnp.int32), axis=2)
    picked = rank[:, :, None] == slots[:, None, :]
    return jnp.sum(jnp.where(picked, key[:, :, None], 0), axis=1)


def band_kernel(key_ref, count_ref, h_ref, a_ref, held, sems):
    block_rows, slot_count = held.shape[:2]
    extra = (slot_count - SURE) // CHUNK

    def part(r, k):
        if k < 0:
            rows = pl.ds(0, SURE)
        else:
            rows = pl.ds(SURE + k * CHUNK, CHUNK)
        return pltpu.make_async_copy(h_ref.at[r, rows], held.at[r, rows], sems.at[r, k + 1])

    def start(r, _):
        part(r, -1).start()
        for k in range(extra):
            pl.when(count_ref[r] > SURE + k * CHUNK)(lambda k=k: part(r, k).start())
        return 0

    lax.fori_loop(0, block_rows, start, 0)

    def one_row(r, _):
        rows = pl.ds(pl.multiple_of(r * B, B), B)
        base = pl.multiple_of((r // 2) * (2 * B), 2 * B)
        a_ref[rows, pl.ds(base, 18 * B)] = jnp.zeros((B, 18 * B), a_ref.dtype)
        part(r, -1).wait()
        for k in range(extra):
            pl.when(count_ref[r] > SURE + k * CHUNK)(lambda k=k: part(r, k).wait())

        def group(g, carry):
            total, last = carry
            for u in range(4):
                key = key_ref[r, g * 4 + u]
                column = key // slot_count
                slot = key % slot_count
                block = held[r, slot].astype(jnp.float32)
                total = jnp.where(column == last, total, 0.0) + block
                last = column
                lanes = pl.ds(pl.multiple_of(column * B, B), B)
                a_ref[rows, lanes] = total.astype(a_ref.dtype)
            return total, last

        groups = (count_ref[r] + 3) // 4
        lax.fori_loop(0, groups, group, (jnp.zeros((B, B), jnp.float32), jnp.int32(-1)))
        return 0

    lax.fori_loop(0, block_rows, one_row, 0)


def build_band(keys, counts, hamiltonian):
    block_rows, slot_count = hamiltonian.shape[:2]
    width = (block_rows + 2 * DIST + 1) * B
    return pl.pallas_call(
        band_kernel,
        out_shape=pltpu.VMEM((block_rows * B, width), jnp.bfloat16),
        in_specs=[
            pl.BlockSpec(memory_space=pltpu.SMEM),
            pl.BlockSpec(memory_space=pltpu.SMEM),
            pl.BlockSpec(memory_space=pltpu.HBM),
        ],
        out_specs=pl.BlockSpec(memory_space=pltpu.VMEM),
        scratch_shapes=[
            pltpu.VMEM(hamiltonian.shape, hamiltonian.dtype),
            pltpu.SemaphoreType.DMA((block_rows, 1 + (slot_count - SURE) // CHUNK)),
        ],
        compiler_params=pltpu.CompilerParams(vmem_limit_bytes=46 * MIB),
        name="band",
    )(keys, counts, hamiltonian)


def own_kernel(v_ref, a_ref, acc_ref):
    rows = acc_ref.shape[1]
    v = v_ref[...]
    for i in range(0, rows, 2 * B):
        acc_ref[:, i : i + 2 * B] = dot_nt(v, a_ref[i : i + 2 * B, DIST * B : DIST * B + rows])


def apply_halo(acc_ref, low_ref, high_ref, a_ref):
    rows = acc_ref.shape[1]
    step = 2 * B
    upper = DIST * B + rows
    for i in range(0, rows, step):
        total = acc_ref[:, i : i + step]
        if i < DIST * B:
            total += dot_nt(low_ref[:, i:], a_ref[i : i + step, i : DIST * B])
        depth = i + step - (rows - DIST * B)
        if depth > 0:
            total += dot_nt(high_ref[:, :depth], a_ref[i : i + step, upper : upper + depth])
        yield i, step, total


def first_kernel(acc_ref, low_ref, high_ref, a_ref, new_ref, top_ref, bottom_ref):
    for i, step, total in apply_halo(acc_ref, low_ref, high_ref, a_ref):
        new_ref[:, i : i + step] = total.astype(new_ref.dtype)
    halos(new_ref, top_ref, bottom_ref)


def halos(new_ref, top_ref, bottom_ref):
    reach = DIST * B
    top_ref[...] = new_ref[:, new_ref.shape[1] - reach :]
    bottom_ref[...] = new_ref[:, :reach]


def next_kernel(acc_ref, low_ref, high_ref, a_ref, older_ref, new_ref, top_ref, bottom_ref):
    for i, step, total in apply_halo(acc_ref, low_ref, high_ref, a_ref):
        older = older_ref[:, i : i + step].astype(jnp.float32)
        new_ref[:, i : i + step] = (2.0 * total - older).astype(new_ref.dtype)
    halos(new_ref, top_ref, bottom_ref)


def image_kernel(acc_ref, low_ref, high_ref, a_ref, new_ref):
    for i, step, total in apply_halo(acc_ref, low_ref, high_ref, a_ref):
        new_ref[:, i : i + step] = total.astype(new_ref.dtype)


def in_vmem(kernel, name, outs, *args, flops=0):
    specs = [pl.BlockSpec(memory_space=pltpu.VMEM)]
    return pl.pallas_call(
        kernel,
        out_shape=[pltpu.VMEM(s, d) for s, d in outs],
        in_specs=specs * len(args),
        out_specs=specs * len(outs),
        compiler_params=pltpu.CompilerParams(vmem_limit_bytes=16 * MIB),
        cost_estimate=pl.CostEstimate(flops=flops, bytes_accessed=0, transcendentals=0),
        name=name,
    )(*args)


def gram_kernel(band_ref, own_ref, other_ref, image_ref, other_image_ref, out_ref):
    own = own_ref[...]
    half = own.shape[0]
    is_first = band_ref[0] == 0

    def both(mine, others):
        a, b = dot_nt(own, mine), dot_nt(own, others)
        return jnp.concatenate([jnp.where(is_first, a, b), jnp.where(is_first, b, a)], axis=1)

    out_ref[:half, :] = both(own, other_ref[...])
    out_ref[half:, :] = both(image_ref[...], other_image_ref[...])


def exchange_halos(top, bottom):
    count = lax.axis_size(ROWS)
    up = [(i, (i + 1) % count) for i in range(count)]
    down = [(target, source) for source, target in up]
    return lax.ppermute(top, ROWS, up), lax.ppermute(bottom, ROWS, down)


def swapped(value, axis, distance):
    count = lax.axis_size(axis)
    return lax.ppermute(value, axis, [(i, i ^ distance) for i in range(count)])


def sum_over_rows(value):
    for axis in ("z", "y", "x"):
        one, two, three = (swapped(value, axis, k) for k in (1, 2, 3))
        value = (value + one) + (two + three)
    return value + swapped(value, "z", 4)


def body(hamiltonian, neighbours, counts, vectors):
    block_rows = hamiltonian.shape[0]
    rows, width = vectors.shape
    reach = DIST * B
    first_block = lax.axis_index(ROWS) * block_rows
    field = ((width, rows), jnp.bfloat16)
    halo = ((width, reach), jnp.bfloat16)
    part = ((width, rows), jnp.float32)
    own_flops = 2 * width * rows * rows

    def own_part(v, name):
        return in_vmem(own_kernel, name, [part], v, band, flops=own_flops)[0]

    start = vectors.T
    low, high = exchange_halos(start[:, rows - reach :], start[:, :reach])
    keys = slot_order(neighbours, counts, first_block)
    band = build_band(keys, counts, hamiltonian)
    acc = own_part(start, "own1")
    level1, top, bottom = in_vmem(first_kernel, "level1", [field, halo, halo], acc, low, high, band)
    older, newer = start, level1
    for degree in range(2, 5):
        low, high = exchange_halos(top, bottom)
        acc = own_part(newer, "own%d" % degree)
        latest, top, bottom = in_vmem(
            next_kernel, "level%d" % degree, [field, halo, halo], acc, low, high, band, older
        )
        older, newer = newer, latest
    low, high = exchange_halos(top, bottom)
    acc = own_part(newer, "own5")
    other = swapped(newer, "band", 1)
    (image,) = in_vmem(image_kernel, "image", [field], acc, low, high, band)
    other_image = swapped(image, "band", 1)
    both = ((2 * width, 2 * width), jnp.float32)
    index = lax.axis_index("band").astype(jnp.int32).reshape(1)
    sums = pl.pallas_call(
        gram_kernel,
        out_shape=jax.ShapeDtypeStruct((2 * width, 2 * width), jnp.float32),
        in_specs=[pl.BlockSpec(memory_space=pltpu.SMEM)]
        + [pl.BlockSpec(memory_space=pltpu.VMEM)] * 4,
        out_specs=pl.BlockSpec(memory_space=pltpu.VMEM),
        compiler_params=pltpu.CompilerParams(vmem_limit_bytes=16 * MIB),
        name="gram",
    )(index, newer, other, image, other_image)
    sums = sum_over_rows(sums) * (1.0 / (rows * lax.axis_size(ROWS)))
    return newer.T, sums[:width], sums[width:]


def solution(mesh):
    shape = tuple(mesh.shape[name] for name in mesh.axis_names)
    chips = Mesh(mesh.devices.reshape(4, 4, 8, shape[1]), (*ROWS, "band"))
    return jax.shard_map(
        body,
        mesh=chips,
        in_specs=(P(ROWS, None, None, None), P(ROWS, None), P(ROWS), P(ROWS, "band")),
        out_specs=(P(ROWS, "band"), P("band", None), P("band", None)),
        check_vma=False,
    )
```

```python
import jax
import jax.numpy as jnp
from jax import lax
from jax.experimental import pallas as pl
from jax.experimental.pallas import tpu as pltpu
from jax.sharding import Mesh, PartitionSpec as P

B = 128
DIST = 8
ROWS = ("x", "y", "z")
UNROLL = 4
NT = (((1,), (1,)), ((), ()))
MIB = 1024 * 1024


def dot_nt(a, b):
    return lax.dot_general(a, b, NT, preferred_element_type=jnp.float32)


def sorted_slots(neighbours, counts):
    block_rows, slot_count = neighbours.shape
    slots = lax.broadcasted_iota(jnp.int32, neighbours.shape, 1)
    square = (block_rows, block_rows)
    own = lax.broadcasted_iota(jnp.int32, square, 0) == lax.broadcasted_iota(jnp.int32, square, 1)
    counts = jnp.sum(jnp.where(own, counts, 0), axis=1, keepdims=True)
    column = neighbours - neighbours[:1, :1] + DIST
    dead = block_rows + 2 * DIST
    key = jnp.where(slots < counts, column, dead) * slot_count + slots
    rank = jnp.zeros_like(key)
    for t in range(slot_count):
        rank += (key[:, t : t + 1] < key).astype(jnp.int32)
    ordered = jnp.zeros_like(key)
    for s in range(slot_count):
        ordered = jnp.where(rank[:, s : s + 1] == slots, key[:, s : s + 1], ordered)
    return ordered, counts


def band_kernel(count_ref, near_ref, h_ref, a_ref, held, staged, key_ref, sems, key_sem):
    block_rows, slot_count = held.shape[:2]

    def part(r):
        return pltpu.make_async_copy(h_ref.at[r], held.at[r], sems.at[r])

    def start(r, _):
        part(r).start()
        return 0

    def clear(r, _):
        base = pl.multiple_of((r // 2) * (2 * B), 2 * B)
        rows = pl.ds(pl.multiple_of(r * B, B), B)
        a_ref[rows, pl.ds(base, 18 * B)] = jnp.zeros((B, 18 * B), a_ref.dtype)
        return 0

    lax.fori_loop(0, block_rows, start, 0)
    ordered, counts = sorted_slots(near_ref[...], count_ref[...])
    staged[:block_rows, :slot_count] = ordered
    staged[:block_rows, slot_count : slot_count + 1] = counts
    keys = pltpu.make_async_copy(staged, key_ref, key_sem)
    keys.start()
    lax.fori_loop(0, block_rows, clear, 0)
    keys.wait()

    def one_row(r, _):
        rows = pl.ds(pl.multiple_of(r * B, B), B)
        part(r).wait()

        def group(g, carry):
            total, last = carry
            for u in range(UNROLL):
                key = key_ref[r, g * UNROLL + u]
                column = key // slot_count
                block = held[r, key % slot_count].astype(jnp.float32)
                total = jnp.where(column == last, total, 0.0) + block
                last = column
                lanes = pl.ds(pl.multiple_of(column * B, B), B)
                a_ref[rows, lanes] = total.astype(a_ref.dtype)
            return total, last

        groups = (key_ref[r, slot_count] + UNROLL - 1) // UNROLL
        lax.fori_loop(0, groups, group, (jnp.zeros((B, B), jnp.float32), jnp.int32(-1)))
        return 0

    lax.fori_loop(0, block_rows, one_row, 0)


def build_band(neighbours, counts, hamiltonian):
    block_rows, slot_count = hamiltonian.shape[:2]
    width = (block_rows + 2 * DIST + 1) * B
    return pl.pallas_call(
        band_kernel,
        out_shape=pltpu.VMEM((block_rows * B, width), jnp.bfloat16),
        in_specs=[
            pl.BlockSpec(memory_space=pltpu.VMEM),
            pl.BlockSpec(memory_space=pltpu.VMEM),
            pl.BlockSpec(memory_space=pltpu.HBM),
        ],
        out_specs=pl.BlockSpec(memory_space=pltpu.VMEM),
        scratch_shapes=[
            pltpu.VMEM(hamiltonian.shape, hamiltonian.dtype),
            pltpu.VMEM((16, B), jnp.int32),
            pltpu.SMEM((16, B), jnp.int32),
            pltpu.SemaphoreType.DMA((block_rows,)),
            pltpu.SemaphoreType.DMA,
        ],
        compiler_params=pltpu.CompilerParams(vmem_limit_bytes=46 * MIB),
        name="band",
    )(counts.reshape(1, block_rows), neighbours, hamiltonian)


def own_kernel(v_ref, a_ref, acc_ref):
    rows = acc_ref.shape[1]
    v = v_ref[...]
    for i in range(0, rows, 2 * B):
        acc_ref[:, i : i + 2 * B] = dot_nt(v, a_ref[i : i + 2 * B, DIST * B : DIST * B + rows])


def apply_halo(acc_ref, low, high, a_ref):
    rows = acc_ref.shape[1]
    step = 2 * B
    upper = DIST * B + rows
    for i in range(0, rows, step):
        total = acc_ref[:, i : i + step]
        if i < DIST * B:
            total += dot_nt(low[:, i:], a_ref[i : i + step, i : DIST * B])
        depth = i + step - (rows - DIST * B)
        if depth > 0:
            total += dot_nt(high[:, :depth], a_ref[i : i + step, upper : upper + depth])
        yield i, step, total


def on_first_core():
    return lax.axis_index("band") == 0


def arrived(there_ref, back_ref):
    there, back = there_ref[...], back_ref[...]
    return jnp.where(on_first_core(), there, back), jnp.where(on_first_core(), back, there)


def depart(new_ref, there_ref, back_ref):
    reach = DIST * B
    top = new_ref[:, new_ref.shape[1] - reach :]
    bottom = new_ref[:, :reach]
    there_ref[...] = jnp.where(on_first_core(), top, bottom)
    back_ref[...] = jnp.where(on_first_core(), bottom, top)


def edges_kernel(new_ref, top_ref, bottom_ref):
    reach = DIST * B
    top_ref[...] = new_ref[:, new_ref.shape[1] - reach :]
    bottom_ref[...] = new_ref[:, :reach]


def first_kernel(acc_ref, low_ref, high_ref, a_ref, new_ref, there_ref, back_ref):
    for i, step, total in apply_halo(acc_ref, low_ref[...], high_ref[...], a_ref):
        new_ref[:, i : i + step] = total.astype(new_ref.dtype)
    depart(new_ref, there_ref, back_ref)


def next_kernel(acc_ref, from_ref, to_ref, a_ref, older_ref, new_ref, there_ref, back_ref):
    for i, step, total in apply_halo(acc_ref, *arrived(from_ref, to_ref), a_ref):
        older = older_ref[:, i : i + step].astype(jnp.float32)
        new_ref[:, i : i + step] = (2.0 * total - older).astype(new_ref.dtype)
    depart(new_ref, there_ref, back_ref)


def image_kernel(acc_ref, from_ref, to_ref, a_ref, new_ref):
    for i, step, total in apply_halo(acc_ref, *arrived(from_ref, to_ref), a_ref):
        new_ref[:, i : i + step] = total.astype(new_ref.dtype)


def in_vmem(kernel, name, outs, *args, flops=0):
    specs = [pl.BlockSpec(memory_space=pltpu.VMEM)]
    return pl.pallas_call(
        kernel,
        out_shape=[pltpu.VMEM(s, d) for s, d in outs],
        in_specs=specs * len(args),
        out_specs=specs * len(outs),
        compiler_params=pltpu.CompilerParams(vmem_limit_bytes=16 * MIB),
        cost_estimate=pl.CostEstimate(flops=flops, bytes_accessed=0, transcendentals=0),
        name=name,
    )(*args)


def gram_kernel(own_ref, other_ref, image_ref, other_image_ref, out_ref):
    own = own_ref[...]
    half = own.shape[0]
    is_first = on_first_core()

    def both(mine, others):
        a, b = dot_nt(own, mine), dot_nt(own, others)
        return jnp.concatenate([jnp.where(is_first, a, b), jnp.where(is_first, b, a)], axis=1)

    out_ref[:half, :] = both(own, other_ref[...])
    out_ref[half:, :] = both(image_ref[...], other_image_ref[...])


def exchange_ring(top, bottom):
    count = lax.axis_size(ROWS)
    up = [(i, (i + 1) % count) for i in range(count)]
    down = [(target, source) for source, target in up]
    return lax.ppermute(top, ROWS, up), lax.ppermute(bottom, ROWS, down)


def exchange_loop(there, back):
    count = lax.axis_size(ROWS)
    loop = [2 * i for i in range(count)] + [2 * i + 1 for i in reversed(range(count))]
    forth = list(zip(loop, loop[1:] + loop[:1]))
    every = (*ROWS, "band")
    return (
        lax.ppermute(there, every, forth),
        lax.ppermute(back, every, [(target, source) for source, target in forth]),
    )


def swapped(value, axis, distance):
    count = lax.axis_size(axis)
    return lax.ppermute(value, axis, [(i, i ^ distance) for i in range(count)])


def sum_over_rows(value):
    for axis, distances in (("z", (1, 2, 3)), ("z", (6,)), ("y", (1, 2, 3)), ("x", (1, 2, 3))):
        own = lax.reduce_precision(value, exponent_bits=8, mantissa_bits=7)
        sent = own.astype(jnp.bfloat16)
        others = [swapped(sent, axis, k).astype(jnp.float32) for k in distances]
        value = own + others[0]
        if len(others) == 3:
            value = value + (others[1] + others[2])
    return value


def body(hamiltonian, neighbours, counts, vectors):
    block_rows = hamiltonian.shape[0]
    rows, width = vectors.shape
    reach = DIST * B
    field = ((width, rows), jnp.bfloat16)
    halo = ((width, reach), jnp.bfloat16)
    part = ((width, rows), jnp.float32)
    own_flops = 2 * width * rows * rows

    def own_part(v, name):
        return in_vmem(own_kernel, name, [part], v, band, flops=own_flops)[0]

    start = vectors.T
    low, high = exchange_ring(*in_vmem(edges_kernel, "edges", [halo, halo], start))
    band = build_band(neighbours, counts, hamiltonian)
    acc = own_part(start, "own1")
    level1, there, back = in_vmem(first_kernel, "level1", [field, halo, halo], acc, low, high, band)
    older, newer = start, level1
    for degree in range(2, 5):
        there, back = exchange_loop(there, back)
        acc = own_part(newer, "own%d" % degree)
        latest, there, back = in_vmem(
            next_kernel, "level%d" % degree, [field, halo, halo], acc, there, back, band, older
        )
        older, newer = newer, latest
    there, back = exchange_loop(there, back)
    acc = own_part(newer, "own5")
    other = swapped(newer, "band", 1)
    (image,) = in_vmem(image_kernel, "image", [field], acc, there, back, band)
    other_image = swapped(image, "band", 1)
    both = ((2 * width, 2 * width), jnp.float32)
    sums = pl.pallas_call(
        gram_kernel,
        out_shape=jax.ShapeDtypeStruct((2 * width, 2 * width), jnp.float32),
        in_specs=[pl.BlockSpec(memory_space=pltpu.VMEM)] * 4,
        out_specs=pl.BlockSpec(memory_space=pltpu.VMEM),
        compiler_params=pltpu.CompilerParams(vmem_limit_bytes=16 * MIB),
        name="gram",
    )(newer, other, image, other_image)
    sums = sum_over_rows(sums) * (1.0 / (rows * lax.axis_size(ROWS)))
    return newer.T, sums[:width], sums[width:]


def solution(mesh):
    shape = tuple(mesh.shape[name] for name in mesh.axis_names)
    chips = Mesh(mesh.devices.reshape(4, 4, 8, shape[1]), (*ROWS, "band"))
    return jax.shard_map(
        body,
        mesh=chips,
        in_specs=(P(ROWS, None, None, None), P(ROWS, None), P(ROWS), P(ROWS, "band")),
        out_specs=(P(ROWS, "band"), P("band", None), P("band", None)),
        check_vma=False,
    )
```

```python
import jax
import jax.numpy as jnp
from jax import lax
from jax.experimental import pallas as pl
from jax.experimental.pallas import tpu as pltpu
from jax.sharding import Mesh, PartitionSpec as P

B = 128
DIST = 8
ROWS = ("x", "y", "z")
UNROLL = 4
NT = (((1,), (1,)), ((), ()))
MIB = 1024 * 1024


def dot_nt(a, b):
    return lax.dot_general(a, b, NT, preferred_element_type=jnp.float32)


def sorted_slots(neighbours, counts):
    block_rows, slot_count = neighbours.shape
    slots = lax.broadcasted_iota(jnp.int32, neighbours.shape, 1)
    square = (block_rows, block_rows)
    own = lax.broadcasted_iota(jnp.int32, square, 0) == lax.broadcasted_iota(jnp.int32, square, 1)
    counts = jnp.sum(jnp.where(own, counts, 0), axis=1, keepdims=True)
    column = neighbours - neighbours[:1, :1] + DIST
    dead = block_rows + 2 * DIST
    key = jnp.where(slots < counts, column, dead) * slot_count + slots
    rank = jnp.zeros_like(key)
    for t in range(slot_count):
        rank += (key[:, t : t + 1] < key).astype(jnp.int32)
    ordered = jnp.zeros_like(key)
    for s in range(slot_count):
        ordered = jnp.where(rank[:, s : s + 1] == slots, key[:, s : s + 1], ordered)
    return ordered, counts


def band_kernel(count_ref, near_ref, h_ref, a_ref, held, staged, key_ref, sems, key_sem):
    block_rows, slot_count = held.shape[:2]

    def part(r):
        return pltpu.make_async_copy(h_ref.at[r], held.at[r], sems.at[r])

    def start(r, _):
        part(r).start()
        return 0

    def clear(r, _):
        base = pl.multiple_of((r // 2) * (2 * B), 2 * B)
        rows = pl.ds(pl.multiple_of(r * B, B), B)
        a_ref[rows, pl.ds(base, 18 * B)] = jnp.zeros((B, 18 * B), a_ref.dtype)
        return 0

    lax.fori_loop(0, block_rows, start, 0)
    ordered, counts = sorted_slots(near_ref[...], count_ref[...])
    staged[:block_rows, :slot_count] = ordered
    staged[:block_rows, slot_count : slot_count + 1] = counts
    keys = pltpu.make_async_copy(staged, key_ref, key_sem)
    keys.start()
    lax.fori_loop(0, block_rows, clear, 0)
    keys.wait()

    def one_row(r, _):
        rows = pl.ds(pl.multiple_of(r * B, B), B)
        part(r).wait()

        def group(g, carry):
            total, last = carry
            for u in range(UNROLL):
                key = key_ref[r, g * UNROLL + u]
                column = key // slot_count
                block = held[r, key % slot_count].astype(jnp.float32)
                total = jnp.where(column == last, total, 0.0) + block
                last = column
                lanes = pl.ds(pl.multiple_of(column * B, B), B)
                a_ref[rows, lanes] = total.astype(a_ref.dtype)
            return total, last

        groups = (key_ref[r, slot_count] + UNROLL - 1) // UNROLL
        lax.fori_loop(0, groups, group, (jnp.zeros((B, B), jnp.float32), jnp.int32(-1)))
        return 0

    lax.fori_loop(0, block_rows, one_row, 0)


def build_band(neighbours, counts, hamiltonian):
    block_rows, slot_count = hamiltonian.shape[:2]
    width = (block_rows + 2 * DIST + 1) * B
    return pl.pallas_call(
        band_kernel,
        out_shape=pltpu.VMEM((block_rows * B, width), jnp.bfloat16),
        in_specs=[
            pl.BlockSpec(memory_space=pltpu.VMEM),
            pl.BlockSpec(memory_space=pltpu.VMEM),
            pl.BlockSpec(memory_space=pltpu.HBM),
        ],
        out_specs=pl.BlockSpec(memory_space=pltpu.VMEM),
        scratch_shapes=[
            pltpu.VMEM(hamiltonian.shape, hamiltonian.dtype),
            pltpu.VMEM((16, B), jnp.int32),
            pltpu.SMEM((16, B), jnp.int32),
            pltpu.SemaphoreType.DMA((block_rows,)),
            pltpu.SemaphoreType.DMA,
        ],
        compiler_params=pltpu.CompilerParams(vmem_limit_bytes=46 * MIB),
        name="band",
    )(counts.reshape(1, block_rows), neighbours, hamiltonian)


def own_kernel(v_ref, a_ref, acc_ref):
    rows = acc_ref.shape[1]
    v = v_ref[...]
    for i in range(0, rows, 2 * B):
        acc_ref[:, i : i + 2 * B] = dot_nt(v, a_ref[i : i + 2 * B, DIST * B : DIST * B + rows])


def apply_halo(acc_ref, low, high, a_ref):
    rows = acc_ref.shape[1]
    step = 2 * B
    upper = DIST * B + rows
    for i in range(0, rows, step):
        total = acc_ref[:, i : i + step]
        if i < DIST * B:
            total += dot_nt(low[:, i:], a_ref[i : i + step, i : DIST * B])
        depth = i + step - (rows - DIST * B)
        if depth > 0:
            total += dot_nt(high[:, :depth], a_ref[i : i + step, upper : upper + depth])
        yield i, step, total


def on_first_core():
    return lax.axis_index("band") == 0


def on_even_chip():
    return lax.axis_index("z") % 2 == 0


def arrived(right_ref, left_ref):
    right, left = right_ref[...], left_ref[...]
    return jnp.where(on_even_chip(), left, right), jnp.where(on_even_chip(), right, left)


def depart(new_ref, right_ref, left_ref):
    reach = DIST * B
    top = new_ref[:, new_ref.shape[1] - reach :]
    bottom = new_ref[:, :reach]
    right_ref[...] = jnp.where(on_even_chip(), top, bottom)
    left_ref[...] = jnp.where(on_even_chip(), bottom, top)


def edges_kernel(new_ref, to_left_ref, to_right_ref):
    depart(new_ref, to_right_ref, to_left_ref)


def first_kernel(acc_ref, right_ref, left_ref, a_ref, new_ref, to_right_ref, to_left_ref):
    for i, step, total in apply_halo(acc_ref, *arrived(right_ref, left_ref), a_ref):
        new_ref[:, i : i + step] = total.astype(new_ref.dtype)
    depart(new_ref, to_right_ref, to_left_ref)


def next_kernel(acc_ref, right_ref, left_ref, a_ref, older_ref, new_ref, to_right_ref, to_left_ref):
    for i, step, total in apply_halo(acc_ref, *arrived(right_ref, left_ref), a_ref):
        older = older_ref[:, i : i + step].astype(jnp.float32)
        new_ref[:, i : i + step] = (2.0 * total - older).astype(new_ref.dtype)
    depart(new_ref, to_right_ref, to_left_ref)


def image_kernel(acc_ref, right_ref, left_ref, a_ref, new_ref):
    for i, step, total in apply_halo(acc_ref, *arrived(right_ref, left_ref), a_ref):
        new_ref[:, i : i + step] = total.astype(new_ref.dtype)


def in_vmem(kernel, name, outs, *args, flops=0):
    specs = [pl.BlockSpec(memory_space=pltpu.VMEM)]
    return pl.pallas_call(
        kernel,
        out_shape=[pltpu.VMEM(s, d) for s, d in outs],
        in_specs=specs * len(args),
        out_specs=specs * len(outs),
        compiler_params=pltpu.CompilerParams(vmem_limit_bytes=16 * MIB),
        cost_estimate=pl.CostEstimate(flops=flops, bytes_accessed=0, transcendentals=0),
        name=name,
    )(*args)


def gram_kernel(own_ref, other_ref, image_ref, other_image_ref, out_ref):
    own = own_ref[...]
    half = own.shape[0]
    is_first = on_first_core()

    def both(mine, others):
        a, b = dot_nt(own, mine), dot_nt(own, others)
        return jnp.concatenate([jnp.where(is_first, a, b), jnp.where(is_first, b, a)], axis=1)

    out_ref[:half, :] = both(own, other_ref[...])
    out_ref[half:, :] = both(image_ref[...], other_image_ref[...])


def exchange(to_right, to_left, left_first=False):
    count = lax.axis_size(ROWS)
    every = (*ROWS, "band")
    pairs = [(i, i + 1) for i in range(0, count, 2)], [(i, i + 1) for i in range(1, count - 1, 2)]
    right, left = [
        [(2 * a + core, 2 * b + core) for core in (0, 1) for i, j in p for a, b in ((i, j), (j, i))]
        for p in pairs
    ]
    for end in (0, count - 1):
        left += [(2 * end, 2 * end + 1), (2 * end + 1, 2 * end)]
    if left_first:
        from_left = lax.ppermute(to_left, every, left)
        return lax.ppermute(to_right, every, right), from_left
    from_right = lax.ppermute(to_right, every, right)
    return from_right, lax.ppermute(to_left, every, left)


def swapped(value, axis, distance):
    count = lax.axis_size(axis)
    return lax.ppermute(value, axis, [(i, i ^ distance) for i in range(count)])


def sum_over_rows(value):
    for axis, distances in (("z", (1, 2, 3)), ("z", (6,)), ("y", (1, 2, 3)), ("x", (1, 2, 3))):
        own = lax.reduce_precision(value, exponent_bits=8, mantissa_bits=7)
        sent = own.astype(jnp.bfloat16)
        others = [swapped(sent, axis, k).astype(jnp.float32) for k in distances]
        value = own + others[0]
        if len(others) == 3:
            value = value + (others[1] + others[2])
    return value


def body(hamiltonian, neighbours, counts, vectors):
    block_rows = hamiltonian.shape[0]
    rows, width = vectors.shape
    reach = DIST * B
    field = ((width, rows), jnp.bfloat16)
    halo = ((width, reach), jnp.bfloat16)
    part = ((width, rows), jnp.float32)
    own_flops = 2 * width * rows * rows

    def own_part(v, name):
        return in_vmem(own_kernel, name, [part], v, band, flops=own_flops)[0]

    start = vectors.T
    to_left, to_right = in_vmem(edges_kernel, "edges", [halo, halo], start)
    right, left = exchange(to_right, to_left, left_first=True)
    band = build_band(neighbours, counts, hamiltonian)
    acc = own_part(start, "own1")
    level1, *edges = in_vmem(first_kernel, "level1", [field, halo, halo], acc, right, left, band)
    older, newer = start, level1
    for degree in range(2, 5):
        right, left = exchange(*edges)
        acc = own_part(newer, "own%d" % degree)
        latest, *edges = in_vmem(
            next_kernel, "level%d" % degree, [field, halo, halo], acc, right, left, band, older
        )
        older, newer = newer, latest
    right, left = exchange(*edges)
    acc, mine = lax.optimization_barrier((own_part(newer, "own5"), newer))
    other = swapped(mine, "band", 1)
    (image,) = in_vmem(image_kernel, "image", [field], acc, right, left, band)
    other_image = swapped(image, "band", 1)
    sums = pl.pallas_call(
        gram_kernel,
        out_shape=jax.ShapeDtypeStruct((2 * width, 2 * width), jnp.float32),
        in_specs=[pl.BlockSpec(memory_space=pltpu.VMEM)] * 4,
        out_specs=pl.BlockSpec(memory_space=pltpu.VMEM),
        compiler_params=pltpu.CompilerParams(vmem_limit_bytes=16 * MIB),
        name="gram",
    )(newer, other, image, other_image)
    sums = sum_over_rows(sums) * (1.0 / (rows * lax.axis_size(ROWS)))
    return newer.T, sums[:width], sums[width:]


def solution(mesh):
    shape = tuple(mesh.shape[name] for name in mesh.axis_names)
    chips = Mesh(mesh.devices.reshape(4, 4, 8, shape[1]), (*ROWS, "band"))
    return jax.shard_map(
        body,
        mesh=chips,
        in_specs=(P(ROWS, None, None, None), P(ROWS, None), P(ROWS), P(ROWS, "band")),
        out_specs=(P(ROWS, "band"), P("band", None), P("band", None)),
        check_vma=False,
    )
```

```python
import jax
import jax.numpy as jnp
from jax import lax
from jax.experimental import pallas as pl
from jax.experimental.pallas import tpu as pltpu
from jax.sharding import Mesh, PartitionSpec as P

B = 128
DIST = 8
ROWS = ("x", "y", "z")
UNROLL = 4
NT = (((1,), (1,)), ((), ()))
MIB = 1024 * 1024


def dot_nt(a, b):
    return lax.dot_general(a, b, NT, preferred_element_type=jnp.float32)


def sorted_slots(neighbours, counts):
    block_rows, slot_count = neighbours.shape
    slots = lax.broadcasted_iota(jnp.int32, neighbours.shape, 1)
    square = (block_rows, block_rows)
    own = lax.broadcasted_iota(jnp.int32, square, 0) == lax.broadcasted_iota(jnp.int32, square, 1)
    counts = jnp.sum(jnp.where(own, counts, 0), axis=1, keepdims=True)
    column = neighbours - neighbours[:1, :1] + DIST
    dead = block_rows + 2 * DIST
    key = jnp.where(slots < counts, column, dead) * slot_count + slots
    rank = jnp.zeros_like(key)
    for t in range(slot_count):
        rank += (key[:, t : t + 1] < key).astype(jnp.int32)
    ordered = jnp.zeros_like(key)
    for s in range(slot_count):
        ordered = jnp.where(rank[:, s : s + 1] == slots, key[:, s : s + 1], ordered)
    return ordered, counts


def band_kernel(count_ref, near_ref, h_ref, a_ref, held, staged, key_ref, sems, key_sem):
    block_rows, slot_count = held.shape[:2]

    def part(r):
        return pltpu.make_async_copy(h_ref.at[r], held.at[r], sems.at[r])

    def start(r, _):
        part(r).start()
        return 0

    def clear(r, _):
        base = pl.multiple_of((r // 2) * (2 * B), 2 * B)
        rows = pl.ds(pl.multiple_of(r * B, B), B)
        a_ref[rows, pl.ds(base, 18 * B)] = jnp.zeros((B, 18 * B), a_ref.dtype)
        return 0

    lax.fori_loop(0, block_rows, start, 0)
    ordered, counts = sorted_slots(near_ref[...], count_ref[...])
    staged[:block_rows, :slot_count] = ordered
    staged[:block_rows, slot_count : slot_count + 1] = counts
    keys = pltpu.make_async_copy(staged, key_ref, key_sem)
    keys.start()
    lax.fori_loop(0, block_rows, clear, 0)
    keys.wait()

    def one_row(r, _):
        rows = pl.ds(pl.multiple_of(r * B, B), B)
        part(r).wait()

        def group(g, carry):
            total, last = carry
            for u in range(UNROLL):
                key = key_ref[r, g * UNROLL + u]
                column = key // slot_count
                block = held[r, key % slot_count].astype(jnp.float32)
                total = jnp.where(column == last, total, 0.0) + block
                last = column
                lanes = pl.ds(pl.multiple_of(column * B, B), B)
                a_ref[rows, lanes] = total.astype(a_ref.dtype)
            return total, last

        groups = (key_ref[r, slot_count] + UNROLL - 1) // UNROLL
        lax.fori_loop(0, groups, group, (jnp.zeros((B, B), jnp.float32), jnp.int32(-1)))
        return 0

    lax.fori_loop(0, block_rows, one_row, 0)


def build_band(neighbours, counts, hamiltonian):
    block_rows, slot_count = hamiltonian.shape[:2]
    width = (block_rows + 2 * DIST + 1) * B
    return pl.pallas_call(
        band_kernel,
        out_shape=pltpu.VMEM((block_rows * B, width), jnp.bfloat16),
        in_specs=[
            pl.BlockSpec(memory_space=pltpu.VMEM),
            pl.BlockSpec(memory_space=pltpu.VMEM),
            pl.BlockSpec(memory_space=pltpu.HBM),
        ],
        out_specs=pl.BlockSpec(memory_space=pltpu.VMEM),
        scratch_shapes=[
            pltpu.VMEM(hamiltonian.shape, hamiltonian.dtype),
            pltpu.VMEM((16, B), jnp.int32),
            pltpu.SMEM((16, B), jnp.int32),
            pltpu.SemaphoreType.DMA((block_rows,)),
            pltpu.SemaphoreType.DMA,
        ],
        compiler_params=pltpu.CompilerParams(vmem_limit_bytes=46 * MIB),
        name="band",
    )(counts.reshape(1, block_rows), neighbours, hamiltonian)


def low_part(low, a_ref, i, step):
    if i >= DIST * B:
        return 0.0
    return dot_nt(low[:, i:], a_ref[i : i + step, i : DIST * B])


def high_part(high, a_ref, i, step):
    upper = a_ref.shape[0] + DIST * B
    depth = i + step - (a_ref.shape[0] - DIST * B)
    if depth <= 0:
        return 0.0
    return dot_nt(high[:, :depth], a_ref[i : i + step, upper : upper + depth])


def near_kernel(v_ref, right_ref, a_ref, acc_ref):
    rows = acc_ref.shape[1]
    step = 2 * B
    v = v_ref[...]

    def run(part):
        halo = right_ref[...]
        for i in range(0, rows, step):
            own = dot_nt(v, a_ref[i : i + step, DIST * B : DIST * B + rows])
            acc_ref[:, i : i + step] = own + part(halo, a_ref, i, step)

    pl.when(on_even_chip())(lambda: run(high_part))
    pl.when(jnp.logical_not(on_even_chip()))(lambda: run(low_part))


def finish(acc_ref, left_ref, a_ref, new_ref, older_ref=None):
    rows = acc_ref.shape[1]
    step = 2 * B

    def run(halo, part):
        for i in range(0, rows, step):
            total = acc_ref[:, i : i + step] + part(halo, a_ref, i, step)
            if older_ref is not None:
                total = 2.0 * total - older_ref[:, i : i + step].astype(jnp.float32)
            new_ref[:, i : i + step] = total.astype(new_ref.dtype)

    reach = DIST * B
    low = left_ref[:, left_ref.shape[1] - reach :]
    high = left_ref[:, :reach]
    pl.when(on_even_chip())(lambda: run(low, low_part))
    pl.when(jnp.logical_not(on_even_chip()))(lambda: run(high, high_part))


def on_first_core():
    return lax.axis_index("band") == 0


def on_even_chip():
    return lax.axis_index("z") % 2 == 0


def depart(new_ref, to_right_ref, to_left_ref):
    reach = DIST * B
    top = new_ref[:, new_ref.shape[1] - reach :]
    bottom = new_ref[:, :reach]
    to_right_ref[...] = jnp.where(on_even_chip(), top, bottom)
    if to_left_ref is not None:
        to_left_ref[...] = jnp.where(on_even_chip(), bottom, top)


def edge_kernel(new_ref, to_right_ref):
    depart(new_ref, to_right_ref, None)


def first_kernel(acc_ref, left_ref, a_ref, new_ref, to_right_ref, to_left_ref):
    finish(acc_ref, left_ref, a_ref, new_ref)
    depart(new_ref, to_right_ref, to_left_ref)


def next_kernel(acc_ref, left_ref, a_ref, older_ref, new_ref, to_right_ref, to_left_ref):
    finish(acc_ref, left_ref, a_ref, new_ref, older_ref)
    depart(new_ref, to_right_ref, to_left_ref)


def image_kernel(acc_ref, left_ref, a_ref, new_ref):
    finish(acc_ref, left_ref, a_ref, new_ref)


def in_vmem(kernel, name, outs, *args, flops=0):
    specs = [pl.BlockSpec(memory_space=pltpu.VMEM)]
    return pl.pallas_call(
        kernel,
        out_shape=[pltpu.VMEM(s, d) for s, d in outs],
        in_specs=specs * len(args),
        out_specs=specs * len(outs),
        compiler_params=pltpu.CompilerParams(vmem_limit_bytes=16 * MIB),
        cost_estimate=pl.CostEstimate(flops=flops, bytes_accessed=0, transcendentals=0),
        name=name,
    )(*args)


def gram_kernel(own_ref, other_ref, image_ref, other_image_ref, out_ref):
    own = own_ref[...]
    half = own.shape[0]
    is_first = on_first_core()

    def both(mine, others):
        a, b = dot_nt(own, mine), dot_nt(own, others)
        return jnp.concatenate([jnp.where(is_first, a, b), jnp.where(is_first, b, a)], axis=1)

    out_ref[:half, :] = both(own, other_ref[...])
    out_ref[half:, :] = both(image_ref[...], other_image_ref[...])


def exchange(to_right, to_left):
    count = lax.axis_size(ROWS)
    every = (*ROWS, "band")
    pairs = [(i, i + 1) for i in range(0, count, 2)], [(i, i + 1) for i in range(1, count - 1, 2)]
    right, left = [
        [(2 * a + core, 2 * b + core) for core in (0, 1) for i, j in p for a, b in ((i, j), (j, i))]
        for p in pairs
    ]
    for end in (0, count - 1):
        left += [(2 * end, 2 * end + 1), (2 * end + 1, 2 * end)]
    return lax.ppermute(to_right, every, right), lax.ppermute(to_left, every, left)


def swapped(value, axis, distance):
    count = lax.axis_size(axis)
    return lax.ppermute(value, axis, [(i, i ^ distance) for i in range(count)])


def sum_over_rows(value):
    for axis, distances in (("z", (1, 2, 3)), ("z", (6,)), ("y", (1, 2, 3)), ("x", (1, 2, 3))):
        own = lax.reduce_precision(value, exponent_bits=8, mantissa_bits=7)
        sent = own.astype(jnp.bfloat16)
        others = [swapped(sent, axis, k).astype(jnp.float32) for k in distances]
        value = own + others[0]
        if len(others) == 3:
            value = value + (others[1] + others[2])
    return value


def body(hamiltonian, neighbours, counts, vectors):
    block_rows = hamiltonian.shape[0]
    rows, width = vectors.shape
    reach = DIST * B
    field = ((width, rows), jnp.bfloat16)
    halo = ((width, reach), jnp.bfloat16)
    part = ((width, rows), jnp.float32)
    near_flops = 3 * width * rows * rows

    def near(v, right, name):
        return in_vmem(near_kernel, name, [part], v, right, band, flops=near_flops)[0]

    start = vectors.T
    right, left = exchange(*in_vmem(edge_kernel, "edge", [halo], start), start)
    band = build_band(neighbours, counts, hamiltonian)
    acc = near(start, right, "near1")
    level1, *edges = in_vmem(first_kernel, "level1", [field, halo, halo], acc, left, band)
    older, newer = start, level1
    for degree in range(2, 5):
        right, left = exchange(*edges)
        acc = near(newer, right, "near%d" % degree)
        latest, *edges = in_vmem(
            next_kernel, "level%d" % degree, [field, halo, halo], acc, left, band, older
        )
        older, newer = newer, latest
    right, left = exchange(*edges)
    acc, mine = lax.optimization_barrier((near(newer, right, "near5"), newer))
    other = swapped(mine, "band", 1)
    (image,) = in_vmem(image_kernel, "image", [field], acc, left, band)
    other_image = swapped(image, "band", 1)
    sums = pl.pallas_call(
        gram_kernel,
        out_shape=jax.ShapeDtypeStruct((2 * width, 2 * width), jnp.float32),
        in_specs=[pl.BlockSpec(memory_space=pltpu.VMEM)] * 4,
        out_specs=pl.BlockSpec(memory_space=pltpu.VMEM),
        compiler_params=pltpu.CompilerParams(vmem_limit_bytes=16 * MIB),
        name="gram",
    )(newer, other, image, other_image)
    sums = sum_over_rows(sums) * (1.0 / (rows * lax.axis_size(ROWS)))
    return newer.T, sums[:width], sums[width:]


def solution(mesh):
    shape = tuple(mesh.shape[name] for name in mesh.axis_names)
    chips = Mesh(mesh.devices.reshape(4, 4, 8, shape[1]), (*ROWS, "band"))
    return jax.shard_map(
        body,
        mesh=chips,
        in_specs=(P(ROWS, None, None, None), P(ROWS, None), P(ROWS), P(ROWS, "band")),
        out_specs=(P(ROWS, "band"), P("band", None), P("band", None)),
        check_vma=False,
    )
```

```python
import jax
import jax.numpy as jnp
from jax import lax
from jax.experimental import pallas as pl
from jax.experimental.pallas import tpu as pltpu
from jax.sharding import Mesh, PartitionSpec as P

B = 128
DIST = 8
ROWS = ("x", "y", "z")
UNROLL = 4
NT = (((1,), (1,)), ((), ()))
MIB = 1024 * 1024


def dot_nt(a, b):
    return lax.dot_general(a, b, NT, preferred_element_type=jnp.float32)


def sorted_slots(neighbours, counts):
    block_rows, slot_count = neighbours.shape
    slots = lax.broadcasted_iota(jnp.int32, neighbours.shape, 1)
    square = (block_rows, block_rows)
    own = lax.broadcasted_iota(jnp.int32, square, 0) == lax.broadcasted_iota(jnp.int32, square, 1)
    counts = jnp.sum(jnp.where(own, counts, 0), axis=1, keepdims=True)
    column = neighbours - neighbours[:1, :1] + DIST
    dead = block_rows + 2 * DIST
    key = jnp.where(slots < counts, column, dead) * slot_count + slots
    rank = jnp.zeros_like(key)
    for t in range(slot_count):
        rank += (key[:, t : t + 1] < key).astype(jnp.int32)
    ordered = jnp.zeros_like(key)
    for s in range(slot_count):
        ordered = jnp.where(rank[:, s : s + 1] == slots, key[:, s : s + 1], ordered)
    return ordered, counts


def band_kernel(count_ref, near_ref, h_ref, a_ref, held, staged, key_ref, sems, key_sem):
    block_rows, slot_count = held.shape[:2]

    def part(r):
        return pltpu.make_async_copy(h_ref.at[r], held.at[r], sems.at[r])

    def start(r, _):
        part(r).start()
        return 0

    def clear(r, _):
        base = pl.multiple_of((r // 2) * (2 * B), 2 * B)
        rows = pl.ds(pl.multiple_of(r * B, B), B)
        a_ref[rows, pl.ds(base, 18 * B)] = jnp.zeros((B, 18 * B), a_ref.dtype)
        return 0

    lax.fori_loop(0, block_rows, start, 0)
    ordered, counts = sorted_slots(near_ref[...], count_ref[...])
    staged[:block_rows, :slot_count] = ordered
    staged[:block_rows, slot_count : slot_count + 1] = counts
    keys = pltpu.make_async_copy(staged, key_ref, key_sem)
    keys.start()
    lax.fori_loop(0, block_rows, clear, 0)
    keys.wait()

    def one_row(r, _):
        rows = pl.ds(pl.multiple_of(r * B, B), B)
        part(r).wait()

        def group(g, carry):
            total, last = carry
            for u in range(UNROLL):
                key = key_ref[r, g * UNROLL + u]
                column = key // slot_count
                block = held[r, key % slot_count].astype(jnp.float32)
                total = jnp.where(column == last, total, 0.0) + block
                last = column
                lanes = pl.ds(pl.multiple_of(column * B, B), B)
                a_ref[rows, lanes] = total.astype(a_ref.dtype)
            return total, last

        groups = (key_ref[r, slot_count] + UNROLL - 1) // UNROLL
        lax.fori_loop(0, groups, group, (jnp.zeros((B, B), jnp.float32), jnp.int32(-1)))
        return 0

    lax.fori_loop(0, block_rows, one_row, 0)


def build_band(neighbours, counts, hamiltonian):
    block_rows, slot_count = hamiltonian.shape[:2]
    width = (block_rows + 2 * DIST + 1) * B
    return pl.pallas_call(
        band_kernel,
        out_shape=pltpu.VMEM((block_rows * B, width), jnp.bfloat16),
        in_specs=[
            pl.BlockSpec(memory_space=pltpu.VMEM),
            pl.BlockSpec(memory_space=pltpu.VMEM),
            pl.BlockSpec(memory_space=pltpu.HBM),
        ],
        out_specs=pl.BlockSpec(memory_space=pltpu.VMEM),
        scratch_shapes=[
            pltpu.VMEM(hamiltonian.shape, hamiltonian.dtype),
            pltpu.VMEM((16, B), jnp.int32),
            pltpu.SMEM((16, B), jnp.int32),
            pltpu.SemaphoreType.DMA((block_rows,)),
            pltpu.SemaphoreType.DMA,
        ],
        compiler_params=pltpu.CompilerParams(vmem_limit_bytes=46 * MIB),
        name="band",
    )(counts.reshape(1, block_rows), neighbours, hamiltonian)


def low_part(low, a_ref, i, step):
    if i >= DIST * B:
        return 0.0
    return dot_nt(low[:, i:], a_ref[i : i + step, i : DIST * B])


def high_part(high, a_ref, i, step):
    upper = a_ref.shape[0] + DIST * B
    depth = i + step - (a_ref.shape[0] - DIST * B)
    if depth <= 0:
        return 0.0
    return dot_nt(high[:, :depth], a_ref[i : i + step, upper : upper + depth])


def halo_sides(ref):
    return ref[:, ref.shape[1] - DIST * B :], ref[:, : DIST * B]


def near_kernel(v_ref, right_ref, a_ref, acc_ref):
    rows = acc_ref.shape[1]
    step = 2 * B
    v = v_ref[...]

    def run(halo, part):
        for i in range(0, rows, step):
            own = dot_nt(v, a_ref[i : i + step, DIST * B : DIST * B + rows])
            acc_ref[:, i : i + step] = own + part(halo, a_ref, i, step)

    low, high = halo_sides(right_ref)
    pl.when(on_even_chip())(lambda: run(high, high_part))
    pl.when(jnp.logical_not(on_even_chip()))(lambda: run(low, low_part))


def finish(acc_ref, left_ref, a_ref, new_ref, older_ref=None):
    rows = acc_ref.shape[1]
    step = 2 * B

    def run(halo, part):
        for i in range(0, rows, step):
            total = acc_ref[:, i : i + step] + part(halo, a_ref, i, step)
            if older_ref is not None:
                total = 2.0 * total - older_ref[:, i : i + step].astype(jnp.float32)
            new_ref[:, i : i + step] = total.astype(new_ref.dtype)

    low, high = halo_sides(left_ref)
    pl.when(on_even_chip())(lambda: run(low, low_part))
    pl.when(jnp.logical_not(on_even_chip()))(lambda: run(high, high_part))


def on_first_core():
    return lax.axis_index("band") == 0


def on_even_chip():
    return lax.axis_index("z") % 2 == 0


def depart(new_ref, to_right_ref, to_left_ref):
    reach = DIST * B
    top = new_ref[:, new_ref.shape[1] - reach :]
    bottom = new_ref[:, :reach]
    to_right_ref[...] = jnp.where(on_even_chip(), top, bottom)
    to_left_ref[...] = jnp.where(on_even_chip(), bottom, top)


def first_kernel(acc_ref, left_ref, a_ref, new_ref, to_right_ref, to_left_ref):
    finish(acc_ref, left_ref, a_ref, new_ref)
    depart(new_ref, to_right_ref, to_left_ref)


def next_kernel(acc_ref, left_ref, a_ref, older_ref, new_ref, to_right_ref, to_left_ref):
    finish(acc_ref, left_ref, a_ref, new_ref, older_ref)
    depart(new_ref, to_right_ref, to_left_ref)


def image_kernel(acc_ref, left_ref, a_ref, new_ref):
    finish(acc_ref, left_ref, a_ref, new_ref)


def in_vmem(kernel, name, outs, *args, flops=0):
    specs = [pl.BlockSpec(memory_space=pltpu.VMEM)]
    return pl.pallas_call(
        kernel,
        out_shape=[pltpu.VMEM(s, d) for s, d in outs],
        in_specs=specs * len(args),
        out_specs=specs * len(outs),
        compiler_params=pltpu.CompilerParams(vmem_limit_bytes=16 * MIB),
        cost_estimate=pl.CostEstimate(flops=flops, bytes_accessed=0, transcendentals=0),
        name=name,
    )(*args)


def gram_kernel(own_ref, other_ref, image_ref, other_image_ref, out_ref):
    own = own_ref[...]
    half = own.shape[0]
    is_first = on_first_core()

    def both(mine, others):
        a, b = dot_nt(own, mine), dot_nt(own, others)
        return jnp.concatenate([jnp.where(is_first, a, b), jnp.where(is_first, b, a)], axis=1)

    out_ref[:half, :] = both(own, other_ref[...])
    out_ref[half:, :] = both(image_ref[...], other_image_ref[...])


def exchange(to_right, to_left):
    count = lax.axis_size(ROWS)
    every = (*ROWS, "band")
    pairs = [(i, i + 1) for i in range(0, count, 2)], [(i, i + 1) for i in range(1, count - 1, 2)]
    right, left = [
        [(2 * a + core, 2 * b + core) for core in (0, 1) for i, j in p for a, b in ((i, j), (j, i))]
        for p in pairs
    ]
    for end in (0, count - 1):
        left += [(2 * end, 2 * end + 1), (2 * end + 1, 2 * end)]
    return lax.ppermute(to_right, every, right), lax.ppermute(to_left, every, left)


def from_other_core(value):
    return lax.ppermute(value, "band", [(0, 1), (1, 0)])


def sum_over_rows(value):
    count = lax.axis_size(ROWS)
    for distances in ((1, 2, 3), (6, 8, 14), (24, 32, 56), (96,)):
        own = lax.reduce_precision(value, exponent_bits=8, mantissa_bits=7)
        sent = own.astype(jnp.bfloat16)
        others = [
            lax.ppermute(sent, ROWS, [(i, i ^ d) for i in range(count)]).astype(jnp.float32)
            for d in distances
        ]
        value = own + others[0]
        if len(others) == 3:
            value = value + (others[1] + others[2])
    return value


def body(hamiltonian, neighbours, counts, vectors):
    block_rows = hamiltonian.shape[0]
    rows, width = vectors.shape
    reach = DIST * B
    field = ((width, rows), jnp.bfloat16)
    halo = ((width, reach), jnp.bfloat16)
    part = ((width, rows), jnp.float32)
    near_flops = 3 * width * rows * rows

    def near(v, right, name):
        return in_vmem(near_kernel, name, [part], v, right, band, flops=near_flops)[0]

    start = vectors.T
    right, left = exchange(start, start)
    band = build_band(neighbours, counts, hamiltonian)
    acc = near(start, right, "near1")
    level1, *edges = in_vmem(first_kernel, "level1", [field, halo, halo], acc, left, band)
    older, newer = start, level1
    for degree in range(2, 5):
        right, left = exchange(*edges)
        acc = near(newer, right, "near%d" % degree)
        latest, *edges = in_vmem(
            next_kernel, "level%d" % degree, [field, halo, halo], acc, left, band, older
        )
        older, newer = newer, latest
    right, left = exchange(*edges)
    acc, mine = lax.optimization_barrier((near(newer, right, "near5"), newer))
    other = from_other_core(mine)
    (image,) = in_vmem(image_kernel, "image", [field], acc, left, band)
    other_image = from_other_core(image)
    sums = pl.pallas_call(
        gram_kernel,
        out_shape=jax.ShapeDtypeStruct((2 * width, 2 * width), jnp.float32),
        in_specs=[pl.BlockSpec(memory_space=pltpu.VMEM)] * 4,
        out_specs=pl.BlockSpec(memory_space=pltpu.VMEM),
        compiler_params=pltpu.CompilerParams(vmem_limit_bytes=16 * MIB),
        name="gram",
    )(newer, other, image, other_image)
    sums = sum_over_rows(sums) * (1.0 / (rows * lax.axis_size(ROWS)))
    return newer.T, sums[:width], sums[width:]


def solution(mesh):
    shape = tuple(mesh.shape[name] for name in mesh.axis_names)
    chips = Mesh(mesh.devices.reshape(4, 4, 8, shape[1]), (*ROWS, "band"))
    return jax.shard_map(
        body,
        mesh=chips,
        in_specs=(P(ROWS, None, None, None), P(ROWS, None), P(ROWS), P(ROWS, "band")),
        out_specs=(P(ROWS, "band"), P("band", None), P("band", None)),
        check_vma=False,
    )
```

```python
import jax
import jax.numpy as jnp
from jax import lax
from jax.experimental import pallas as pl
from jax.experimental.pallas import tpu as pltpu
from jax.sharding import Mesh, PartitionSpec as P

B = 128
DIST = 8
ROWS = ("x", "y", "z")
UNROLL = 4
NT = (((1,), (1,)), ((), ()))
MIB = 1024 * 1024


def dot_nt(a, b):
    return lax.dot_general(a, b, NT, preferred_element_type=jnp.float32)


def sorted_slots(neighbours, counts):
    block_rows, slot_count = neighbours.shape
    slots = lax.broadcasted_iota(jnp.int32, neighbours.shape, 1)
    square = (block_rows, block_rows)
    own = lax.broadcasted_iota(jnp.int32, square, 0) == lax.broadcasted_iota(jnp.int32, square, 1)
    counts = jnp.sum(jnp.where(own, counts, 0), axis=1, keepdims=True)
    column = neighbours - neighbours[:1, :1] + DIST
    dead = block_rows + 2 * DIST
    key = jnp.where(slots < counts, column, dead) * slot_count + slots
    rank = jnp.zeros_like(key)
    for t in range(slot_count):
        rank += (key[:, t : t + 1] < key).astype(jnp.int32)
    ordered = jnp.zeros_like(key)
    for s in range(slot_count):
        ordered = jnp.where(rank[:, s : s + 1] == slots, key[:, s : s + 1], ordered)
    return ordered, counts


def band_kernel(count_ref, near_ref, h_ref, a_ref, held, staged, key_ref, sems, key_sem):
    block_rows, slot_count = held.shape[:2]

    def part(r):
        return pltpu.make_async_copy(h_ref.at[r], held.at[r], sems.at[r])

    def start(r, _):
        part(r).start()
        return 0

    def clear(r, _):
        base = pl.multiple_of((r // 2) * (2 * B), 2 * B)
        rows = pl.ds(pl.multiple_of(r * B, B), B)
        a_ref[rows, pl.ds(base, 18 * B)] = jnp.zeros((B, 18 * B), a_ref.dtype)
        return 0

    lax.fori_loop(0, block_rows, start, 0)
    ordered, counts = sorted_slots(near_ref[...], count_ref[...])
    staged[:block_rows, :slot_count] = ordered
    staged[:block_rows, slot_count : slot_count + 1] = counts
    keys = pltpu.make_async_copy(staged, key_ref, key_sem)
    keys.start()
    lax.fori_loop(0, block_rows, clear, 0)
    keys.wait()

    def one_row(r, _):
        rows = pl.ds(pl.multiple_of(r * B, B), B)
        part(r).wait()

        def group(g, carry):
            total, last = carry
            for u in range(UNROLL):
                key = key_ref[r, g * UNROLL + u]
                column = key // slot_count
                block = held[r, key % slot_count].astype(jnp.float32)
                total = jnp.where(column == last, total, 0.0) + block
                last = column
                lanes = pl.ds(pl.multiple_of(column * B, B), B)
                a_ref[rows, lanes] = total.astype(a_ref.dtype)
            return total, last

        groups = (key_ref[r, slot_count] + UNROLL - 1) // UNROLL
        lax.fori_loop(0, groups, group, (jnp.zeros((B, B), jnp.float32), jnp.int32(-1)))
        return 0

    lax.fori_loop(0, block_rows, one_row, 0)


def build_band(neighbours, counts, hamiltonian):
    block_rows, slot_count = hamiltonian.shape[:2]
    width = (block_rows + 2 * DIST + 1) * B
    return pl.pallas_call(
        band_kernel,
        out_shape=pltpu.VMEM((block_rows * B, width), jnp.bfloat16),
        in_specs=[
            pl.BlockSpec(memory_space=pltpu.VMEM),
            pl.BlockSpec(memory_space=pltpu.VMEM),
            pl.BlockSpec(memory_space=pltpu.HBM),
        ],
        out_specs=pl.BlockSpec(memory_space=pltpu.VMEM),
        scratch_shapes=[
            pltpu.VMEM(hamiltonian.shape, hamiltonian.dtype),
            pltpu.VMEM((16, B), jnp.int32),
            pltpu.SMEM((16, B), jnp.int32),
            pltpu.SemaphoreType.DMA((block_rows,)),
            pltpu.SemaphoreType.DMA,
        ],
        compiler_params=pltpu.CompilerParams(vmem_limit_bytes=46 * MIB),
        name="band",
    )(counts.reshape(1, block_rows), neighbours, hamiltonian)


def low_part(low, a_ref, i, step):
    if i >= DIST * B:
        return 0.0
    return dot_nt(low[:, i:], a_ref[i : i + step, i : DIST * B])


def high_part(high, a_ref, i, step):
    upper = a_ref.shape[0] + DIST * B
    depth = i + step - (a_ref.shape[0] - DIST * B)
    if depth <= 0:
        return 0.0
    return dot_nt(high[:, :depth], a_ref[i : i + step, upper : upper + depth])


def halo_sides(ref):
    return ref[:, ref.shape[1] - DIST * B :], ref[:, : DIST * B]


def near_kernel(v_ref, right_ref, a_ref, acc_ref, older_ref=None):
    rows = acc_ref.shape[1]
    step = 2 * B
    v = v_ref[...]

    def run(halo, part):
        for i in range(0, rows, step):
            total = dot_nt(v, a_ref[i : i + step, DIST * B : DIST * B + rows])
            total += part(halo, a_ref, i, step)
            if older_ref is not None:
                total = 2.0 * total - older_ref[:, i : i + step].astype(jnp.float32)
            acc_ref[:, i : i + step] = total

    low, high = halo_sides(right_ref)
    pl.when(on_even_chip())(lambda: run(high, high_part))
    pl.when(jnp.logical_not(on_even_chip()))(lambda: run(low, low_part))


def near_next_kernel(v_ref, right_ref, a_ref, older_ref, acc_ref):
    near_kernel(v_ref, right_ref, a_ref, acc_ref, older_ref)


def finish(acc_ref, left_ref, a_ref, new_ref, scale=1.0):
    rows = acc_ref.shape[1]
    step = 2 * B

    def run(halo, part):
        for i in range(0, rows, step):
            total = acc_ref[:, i : i + step] + scale * part(halo, a_ref, i, step)
            new_ref[:, i : i + step] = total.astype(new_ref.dtype)

    low, high = halo_sides(left_ref)
    pl.when(on_even_chip())(lambda: run(low, low_part))
    pl.when(jnp.logical_not(on_even_chip()))(lambda: run(high, high_part))


def on_first_core():
    return lax.axis_index("band") == 0


def on_even_chip():
    return lax.axis_index("z") % 2 == 0


def depart(new_ref, to_right_ref, to_left_ref):
    reach = DIST * B
    top = new_ref[:, new_ref.shape[1] - reach :]
    bottom = new_ref[:, :reach]
    to_right_ref[...] = jnp.where(on_even_chip(), top, bottom)
    to_left_ref[...] = jnp.where(on_even_chip(), bottom, top)


def first_kernel(acc_ref, left_ref, a_ref, new_ref, to_right_ref, to_left_ref):
    finish(acc_ref, left_ref, a_ref, new_ref)
    depart(new_ref, to_right_ref, to_left_ref)


def next_kernel(acc_ref, left_ref, a_ref, new_ref, to_right_ref, to_left_ref):
    finish(acc_ref, left_ref, a_ref, new_ref, 2.0)
    depart(new_ref, to_right_ref, to_left_ref)


def image_kernel(acc_ref, left_ref, a_ref, new_ref):
    finish(acc_ref, left_ref, a_ref, new_ref)


def in_vmem(kernel, name, outs, *args, flops=0):
    specs = [pl.BlockSpec(memory_space=pltpu.VMEM)]
    return pl.pallas_call(
        kernel,
        out_shape=[pltpu.VMEM(s, d) for s, d in outs],
        in_specs=specs * len(args),
        out_specs=specs * len(outs),
        compiler_params=pltpu.CompilerParams(vmem_limit_bytes=16 * MIB),
        cost_estimate=pl.CostEstimate(flops=flops, bytes_accessed=0, transcendentals=0),
        name=name,
    )(*args)


def gram_kernel(own_ref, other_ref, image_ref, other_image_ref, out_ref):
    own = own_ref[...]
    half = own.shape[0]
    is_first = on_first_core()

    def both(mine, others):
        a, b = dot_nt(own, mine), dot_nt(own, others)
        return jnp.concatenate([jnp.where(is_first, a, b), jnp.where(is_first, b, a)], axis=1)

    out_ref[:half, :] = both(own, other_ref[...])
    out_ref[half:, :] = both(image_ref[...], other_image_ref[...])


def exchange(to_right, to_left):
    count = lax.axis_size(ROWS)
    every = (*ROWS, "band")
    pairs = [(i, i + 1) for i in range(0, count, 2)], [(i, i + 1) for i in range(1, count - 1, 2)]
    right, left = [
        [(2 * a + core, 2 * b + core) for core in (0, 1) for i, j in p for a, b in ((i, j), (j, i))]
        for p in pairs
    ]
    for end in (0, count - 1):
        left += [(2 * end, 2 * end + 1), (2 * end + 1, 2 * end)]
    return lax.ppermute(to_right, every, right), lax.ppermute(to_left, every, left)


def from_other_core(value):
    return lax.ppermute(value, "band", [(0, 1), (1, 0)])


def sum_over_rows(value):
    count = lax.axis_size(ROWS)
    for distances in ((1, 2, 3), (6,), (8, 16, 24), (32, 64, 96)):
        own = lax.reduce_precision(value, exponent_bits=8, mantissa_bits=7)
        sent = own.astype(jnp.bfloat16)
        others = [
            lax.ppermute(sent, ROWS, [(i, i ^ d) for i in range(count)]).astype(jnp.float32)
            for d in distances
        ]
        value = own + others[0]
        if len(others) == 3:
            value = value + (others[1] + others[2])
    return value


def body(hamiltonian, neighbours, counts, vectors):
    block_rows = hamiltonian.shape[0]
    rows, width = vectors.shape
    reach = DIST * B
    field = ((width, rows), jnp.bfloat16)
    halo = ((width, reach), jnp.bfloat16)
    part = ((width, rows), jnp.float32)
    near_flops = 3 * width * rows * rows

    def near(v, right, name, *older):
        kernel = near_next_kernel if older else near_kernel
        return in_vmem(kernel, name, [part], v, right, band, *older, flops=near_flops)[0]

    start = vectors.T
    right, left = exchange(start, start)
    band = build_band(neighbours, counts, hamiltonian)
    acc = near(start, right, "near1")
    level1, *edges = in_vmem(first_kernel, "level1", [field, halo, halo], acc, left, band)
    older, newer = start, level1
    for degree in range(2, 5):
        right, left = exchange(*edges)
        acc = near(newer, right, "near%d" % degree, older)
        latest, *edges = in_vmem(
            next_kernel, "level%d" % degree, [field, halo, halo], acc, left, band
        )
        older, newer = newer, latest
    right, left = exchange(*edges)
    acc, mine = lax.optimization_barrier((near(newer, right, "near5"), newer))
    other = from_other_core(mine)
    (image,) = in_vmem(image_kernel, "image", [field], acc, left, band)
    other_image = from_other_core(image)
    sums = pl.pallas_call(
        gram_kernel,
        out_shape=jax.ShapeDtypeStruct((2 * width, 2 * width), jnp.float32),
        in_specs=[pl.BlockSpec(memory_space=pltpu.VMEM)] * 4,
        out_specs=pl.BlockSpec(memory_space=pltpu.VMEM),
        compiler_params=pltpu.CompilerParams(vmem_limit_bytes=16 * MIB),
        name="gram",
    )(newer, other, image, other_image)
    sums = sum_over_rows(sums) * (1.0 / (rows * lax.axis_size(ROWS)))
    return newer.T, sums[:width], sums[width:]


def solution(mesh):
    shape = tuple(mesh.shape[name] for name in mesh.axis_names)
    chips = Mesh(mesh.devices.reshape(4, 4, 8, shape[1]), (*ROWS, "band"))
    return jax.shard_map(
        body,
        mesh=chips,
        in_specs=(P(ROWS, None, None, None), P(ROWS, None), P(ROWS), P(ROWS, "band")),
        out_specs=(P(ROWS, "band"), P("band", None), P("band", None)),
        check_vma=False,
    )
```

```python
import jax
import jax.numpy as jnp
from jax import lax
from jax.experimental import pallas as pl
from jax.experimental.pallas import tpu as pltpu
from jax.sharding import Mesh, PartitionSpec as P

B = 128
DIST = 8
ROWS = ("x", "y", "z")
UNROLL = 4
NT = (((1,), (1,)), ((), ()))
MIB = 1024 * 1024


def dot_nt(a, b):
    return lax.dot_general(a, b, NT, preferred_element_type=jnp.float32)


def sorted_slots(neighbours, counts):
    block_rows, slot_count = neighbours.shape
    slots = lax.broadcasted_iota(jnp.int32, neighbours.shape, 1)
    square = (block_rows, block_rows)
    own = lax.broadcasted_iota(jnp.int32, square, 0) == lax.broadcasted_iota(jnp.int32, square, 1)
    counts = jnp.sum(jnp.where(own, counts, 0), axis=1, keepdims=True)
    column = neighbours - neighbours[:1, :1] + DIST
    dead = block_rows + 2 * DIST
    key = jnp.where(slots < counts, column, dead) * slot_count + slots
    rank = jnp.zeros_like(key)
    for t in range(slot_count):
        rank += (key[:, t : t + 1] < key).astype(jnp.int32)
    ordered = jnp.zeros_like(key)
    for s in range(slot_count):
        ordered = jnp.where(rank[:, s : s + 1] == slots, key[:, s : s + 1], ordered)
    return ordered, counts


def band_kernel(count_ref, near_ref, h_ref, a_ref, held, staged, key_ref, sems, key_sem):
    block_rows, slot_count = held.shape[:2]

    def part(r):
        return pltpu.make_async_copy(h_ref.at[r], held.at[r], sems.at[r])

    def start(r, _):
        part(r).start()
        return 0

    def clear(r, _):
        base = pl.multiple_of((r // 2) * (2 * B), 2 * B)
        rows = pl.ds(pl.multiple_of(r * B, B), B)
        a_ref[rows, pl.ds(base, 18 * B)] = jnp.zeros((B, 18 * B), a_ref.dtype)
        return 0

    lax.fori_loop(0, block_rows, start, 0)
    ordered, counts = sorted_slots(near_ref[...], count_ref[...])
    staged[:block_rows, :slot_count] = ordered
    staged[:block_rows, slot_count : slot_count + 1] = counts
    keys = pltpu.make_async_copy(staged, key_ref, key_sem)
    keys.start()
    lax.fori_loop(0, block_rows, clear, 0)
    keys.wait()

    def one_row(r, _):
        rows = pl.ds(pl.multiple_of(r * B, B), B)
        part(r).wait()

        def group(g, carry):
            total, last = carry
            for u in range(UNROLL):
                key = key_ref[r, g * UNROLL + u]
                column = key // slot_count
                block = held[r, key % slot_count].astype(jnp.float32)
                total = jnp.where(column == last, total, 0.0) + block
                last = column
                lanes = pl.ds(pl.multiple_of(column * B, B), B)
                a_ref[rows, lanes] = total.astype(a_ref.dtype)
            return total, last

        groups = (key_ref[r, slot_count] + UNROLL - 1) // UNROLL
        lax.fori_loop(0, groups, group, (jnp.zeros((B, B), jnp.float32), jnp.int32(-1)))
        return 0

    lax.fori_loop(0, block_rows, one_row, 0)


def build_band(neighbours, counts, hamiltonian):
    block_rows, slot_count = hamiltonian.shape[:2]
    width = (block_rows + 2 * DIST + 1) * B
    return pl.pallas_call(
        band_kernel,
        out_shape=pltpu.VMEM((block_rows * B, width), jnp.bfloat16),
        in_specs=[
            pl.BlockSpec(memory_space=pltpu.VMEM),
            pl.BlockSpec(memory_space=pltpu.VMEM),
            pl.BlockSpec(memory_space=pltpu.HBM),
        ],
        out_specs=pl.BlockSpec(memory_space=pltpu.VMEM),
        scratch_shapes=[
            pltpu.VMEM(hamiltonian.shape, hamiltonian.dtype),
            pltpu.VMEM((16, B), jnp.int32),
            pltpu.SMEM((16, B), jnp.int32),
            pltpu.SemaphoreType.DMA((block_rows,)),
            pltpu.SemaphoreType.DMA,
        ],
        compiler_params=pltpu.CompilerParams(vmem_limit_bytes=46 * MIB),
        name="band",
    )(counts.reshape(1, block_rows), neighbours, hamiltonian)


def low_part(low, a_ref, i, step):
    if i >= DIST * B:
        return 0.0
    return dot_nt(low[:, i:], a_ref[i : i + step, i : DIST * B])


def high_part(high, a_ref, i, step):
    upper = a_ref.shape[0] + DIST * B
    depth = i + step - (a_ref.shape[0] - DIST * B)
    if depth <= 0:
        return 0.0
    return dot_nt(high[:, :depth], a_ref[i : i + step, upper : upper + depth])


def halo_sides(ref):
    return ref[:, ref.shape[1] - DIST * B :], ref[:, : DIST * B]


def near_kernel(v_ref, right_ref, a_ref, acc_ref, older_ref=None):
    rows = acc_ref.shape[1]
    step = 2 * B
    v = v_ref[...]

    def run(halo, part):
        for i in range(0, rows, step):
            total = dot_nt(v, a_ref[i : i + step, DIST * B : DIST * B + rows])
            total += part(halo, a_ref, i, step)
            if older_ref is not None:
                total = 2.0 * total - older_ref[:, i : i + step].astype(jnp.float32)
            acc_ref[:, i : i + step] = total

    low, high = halo_sides(right_ref)
    pl.when(on_even_chip())(lambda: run(high, high_part))
    pl.when(jnp.logical_not(on_even_chip()))(lambda: run(low, low_part))


def near_next_kernel(v_ref, right_ref, a_ref, older_ref, acc_ref):
    near_kernel(v_ref, right_ref, a_ref, acc_ref, older_ref)


def finish(acc_ref, left_ref, a_ref, new_ref, scale=1.0):
    rows = acc_ref.shape[1]
    step = 2 * B

    def run(halo, part):
        for i in range(0, rows, step):
            total = acc_ref[:, i : i + step] + scale * part(halo, a_ref, i, step)
            new_ref[:, i : i + step] = total.astype(new_ref.dtype)

    low, high = halo_sides(left_ref)
    pl.when(on_even_chip())(lambda: run(low, low_part))
    pl.when(jnp.logical_not(on_even_chip()))(lambda: run(high, high_part))


def on_first_core():
    return lax.axis_index("band") == 0


def on_even_chip():
    return lax.axis_index("z") % 2 == 0


def depart(new_ref, to_right_ref, to_left_ref):
    reach = DIST * B
    top = new_ref[:, new_ref.shape[1] - reach :]
    bottom = new_ref[:, :reach]
    to_right_ref[...] = jnp.where(on_even_chip(), top, bottom)
    to_left_ref[...] = jnp.where(on_even_chip(), bottom, top)


def first_kernel(acc_ref, left_ref, a_ref, new_ref, to_right_ref, to_left_ref):
    finish(acc_ref, left_ref, a_ref, new_ref)
    depart(new_ref, to_right_ref, to_left_ref)


def next_kernel(acc_ref, left_ref, a_ref, new_ref, to_right_ref, to_left_ref):
    finish(acc_ref, left_ref, a_ref, new_ref, 2.0)
    depart(new_ref, to_right_ref, to_left_ref)


def image_kernel(acc_ref, left_ref, a_ref, new_ref):
    finish(acc_ref, left_ref, a_ref, new_ref)


def in_vmem(kernel, name, outs, *args, flops=0):
    specs = [pl.BlockSpec(memory_space=pltpu.VMEM)]
    return pl.pallas_call(
        kernel,
        out_shape=[pltpu.VMEM(s, d) for s, d in outs],
        in_specs=specs * len(args),
        out_specs=specs * len(outs),
        compiler_params=pltpu.CompilerParams(vmem_limit_bytes=16 * MIB),
        cost_estimate=pl.CostEstimate(flops=flops, bytes_accessed=0, transcendentals=0),
        name=name,
    )(*args)


def gram_kernel(own_ref, other_ref, image_ref, other_image_ref, out_ref):
    own = own_ref[...]
    half = own.shape[0]
    is_first = on_first_core()

    def both(mine, others):
        a, b = dot_nt(own, mine), dot_nt(own, others)
        return jnp.concatenate([jnp.where(is_first, a, b), jnp.where(is_first, b, a)], axis=1)

    out_ref[:half, :] = both(own, other_ref[...])
    out_ref[half:, :] = both(image_ref[...], other_image_ref[...])


def exchange(to_right, to_left):
    count = lax.axis_size(ROWS)
    every = (*ROWS, "band")
    pairs = [(i, i + 1) for i in range(0, count, 2)], [(i, i + 1) for i in range(1, count - 1, 2)]
    right, left = [
        [(2 * a + core, 2 * b + core) for core in (0, 1) for i, j in p for a, b in ((i, j), (j, i))]
        for p in pairs
    ]
    for end in (0, count - 1):
        left += [(2 * end, 2 * end + 1), (2 * end + 1, 2 * end)]
    return lax.ppermute(to_right, every, right), lax.ppermute(to_left, every, left)


def from_other_core(value):
    return lax.ppermute(value, "band", [(0, 1), (1, 0)])


def sum_over_rows(value):
    count = lax.axis_size(ROWS)
    for distances in ((7,), (1, 2, 3), (8, 16, 24), (32, 64, 96)):
        own = lax.reduce_precision(value, exponent_bits=8, mantissa_bits=7)
        sent = own.astype(jnp.bfloat16)
        others = [
            lax.ppermute(sent, ROWS, [(i, i ^ d) for i in range(count)]).astype(jnp.float32)
            for d in distances
        ]
        value = own + others[0]
        if len(others) == 3:
            value = value + (others[1] + others[2])
    return value


def body(hamiltonian, neighbours, counts, vectors):
    block_rows = hamiltonian.shape[0]
    rows, width = vectors.shape
    reach = DIST * B
    field = ((width, rows), jnp.bfloat16)
    halo = ((width, reach), jnp.bfloat16)
    part = ((width, rows), jnp.float32)
    near_flops = 3 * width * rows * rows

    def near(v, right, name, *older):
        kernel = near_next_kernel if older else near_kernel
        return in_vmem(kernel, name, [part], v, right, band, *older, flops=near_flops)[0]

    start = vectors.T
    right, left = exchange(start, start)
    band = build_band(neighbours, counts, hamiltonian)
    acc = near(start, right, "near1")
    level1, *edges = in_vmem(first_kernel, "level1", [field, halo, halo], acc, left, band)
    older, newer = start, level1
    for degree in range(2, 5):
        right, left = exchange(*edges)
        acc = near(newer, right, "near%d" % degree, older)
        latest, *edges = in_vmem(
            next_kernel, "level%d" % degree, [field, halo, halo], acc, left, band
        )
        older, newer = newer, latest
    right, left = exchange(*edges)
    acc, mine = lax.optimization_barrier((near(newer, right, "near5"), newer))
    other = from_other_core(mine)
    (image,) = in_vmem(image_kernel, "image", [field], acc, left, band)
    other_image = from_other_core(image)
    sums = pl.pallas_call(
        gram_kernel,
        out_shape=jax.ShapeDtypeStruct((2 * width, 2 * width), jnp.float32),
        in_specs=[pl.BlockSpec(memory_space=pltpu.VMEM)] * 4,
        out_specs=pl.BlockSpec(memory_space=pltpu.VMEM),
        compiler_params=pltpu.CompilerParams(vmem_limit_bytes=16 * MIB),
        name="gram",
    )(newer, other, image, other_image)
    sums = sum_over_rows(sums) * (1.0 / (rows * lax.axis_size(ROWS)))
    return newer.T, sums[:width], sums[width:]


def solution(mesh):
    shape = tuple(mesh.shape[name] for name in mesh.axis_names)
    chips = Mesh(mesh.devices.reshape(4, 4, 8, shape[1]), (*ROWS, "band"))
    return jax.shard_map(
        body,
        mesh=chips,
        in_specs=(P(ROWS, None, None, None), P(ROWS, None), P(ROWS), P(ROWS, "band")),
        out_specs=(P(ROWS, "band"), P("band", None), P("band", None)),
        check_vma=False,
    )
```

```python
import jax
import jax.numpy as jnp
from jax import lax
from jax.experimental import pallas as pl
from jax.experimental.pallas import tpu as pltpu
from jax.sharding import Mesh, PartitionSpec as P

B = 128
DIST = 8
ROWS = ("x", "y", "z")
UNROLL = 4
NT = (((1,), (1,)), ((), ()))
MIB = 1024 * 1024


def dot_nt(a, b):
    return lax.dot_general(a, b, NT, preferred_element_type=jnp.float32)


def sorted_slots(neighbours, counts):
    block_rows, slot_count = neighbours.shape
    slots = lax.broadcasted_iota(jnp.int32, neighbours.shape, 1)
    square = (block_rows, block_rows)
    own = lax.broadcasted_iota(jnp.int32, square, 0) == lax.broadcasted_iota(jnp.int32, square, 1)
    counts = jnp.sum(jnp.where(own, counts, 0), axis=1, keepdims=True)
    column = neighbours - neighbours[:1, :1] + DIST
    dead = block_rows + 2 * DIST
    key = jnp.where(slots < counts, column, dead) * slot_count + slots
    rank = jnp.zeros_like(key)
    for t in range(slot_count):
        rank += (key[:, t : t + 1] < key).astype(jnp.int32)
    ordered = jnp.zeros_like(key)
    for s in range(slot_count):
        ordered = jnp.where(rank[:, s : s + 1] == slots, key[:, s : s + 1], ordered)
    return ordered, counts


def band_kernel(count_ref, near_ref, h_ref, a_ref, held, staged, key_ref, sems, key_sem):
    block_rows, slot_count = held.shape[:2]

    def part(r):
        return pltpu.make_async_copy(h_ref.at[r], held.at[r], sems.at[r])

    def start(r, _):
        part(r).start()
        return 0

    def clear(r, _):
        base = pl.multiple_of((r // 2) * (2 * B), 2 * B)
        rows = pl.ds(pl.multiple_of(r * B, B), B)
        a_ref[rows, pl.ds(base, 18 * B)] = jnp.zeros((B, 18 * B), a_ref.dtype)
        return 0

    lax.fori_loop(0, block_rows, start, 0)
    ordered, counts = sorted_slots(near_ref[...], count_ref[...])
    staged[:block_rows, :slot_count] = ordered
    staged[:block_rows, slot_count : slot_count + 1] = counts
    keys = pltpu.make_async_copy(staged, key_ref, key_sem)
    keys.start()
    lax.fori_loop(0, block_rows, clear, 0)
    keys.wait()

    def one_row(r, _):
        rows = pl.ds(pl.multiple_of(r * B, B), B)
        part(r).wait()

        def group(g, carry):
            total, last = carry
            for u in range(UNROLL):
                key = key_ref[r, g * UNROLL + u]
                column = key // slot_count
                block = held[r, key % slot_count].astype(jnp.float32)
                total = jnp.where(column == last, total, 0.0) + block
                last = column
                lanes = pl.ds(pl.multiple_of(column * B, B), B)
                a_ref[rows, lanes] = total.astype(a_ref.dtype)
            return total, last

        groups = (key_ref[r, slot_count] + UNROLL - 1) // UNROLL
        lax.fori_loop(0, groups, group, (jnp.zeros((B, B), jnp.float32), jnp.int32(-1)))
        return 0

    lax.fori_loop(0, block_rows, one_row, 0)


def build_band(neighbours, counts, hamiltonian):
    block_rows, slot_count = hamiltonian.shape[:2]
    width = (block_rows + 2 * DIST + 1) * B
    return pl.pallas_call(
        band_kernel,
        out_shape=pltpu.VMEM((block_rows * B, width), jnp.bfloat16),
        in_specs=[
            pl.BlockSpec(memory_space=pltpu.VMEM),
            pl.BlockSpec(memory_space=pltpu.VMEM),
            pl.BlockSpec(memory_space=pltpu.HBM),
        ],
        out_specs=pl.BlockSpec(memory_space=pltpu.VMEM),
        scratch_shapes=[
            pltpu.VMEM(hamiltonian.shape, hamiltonian.dtype),
            pltpu.VMEM((16, B), jnp.int32),
            pltpu.SMEM((16, B), jnp.int32),
            pltpu.SemaphoreType.DMA((block_rows,)),
            pltpu.SemaphoreType.DMA,
        ],
        compiler_params=pltpu.CompilerParams(vmem_limit_bytes=46 * MIB),
        name="band",
    )(counts.reshape(1, block_rows), neighbours, hamiltonian)


def low_part(low, a_ref, i, step):
    if i >= DIST * B:
        return 0.0
    return dot_nt(low[:, i:], a_ref[i : i + step, i : DIST * B])


def high_part(high, a_ref, i, step):
    upper = a_ref.shape[0] + DIST * B
    depth = i + step - (a_ref.shape[0] - DIST * B)
    if depth <= 0:
        return 0.0
    return dot_nt(high[:, :depth], a_ref[i : i + step, upper : upper + depth])


def halo_sides(ref):
    return ref[:, ref.shape[1] - DIST * B :], ref[:, : DIST * B]


def near_kernel(v_ref, right_ref, a_ref, acc_ref, older_ref=None):
    rows = acc_ref.shape[1]
    step = 2 * B
    v = v_ref[...]

    def run(halo, part):
        for i in range(0, rows, step):
            total = dot_nt(v, a_ref[i : i + step, DIST * B : DIST * B + rows])
            total += part(halo, a_ref, i, step)
            if older_ref is not None:
                total = 2.0 * total - older_ref[:, i : i + step].astype(jnp.float32)
            acc_ref[:, i : i + step] = total

    low, high = halo_sides(right_ref)
    pl.when(on_even_chip())(lambda: run(high, high_part))
    pl.when(jnp.logical_not(on_even_chip()))(lambda: run(low, low_part))


def near_next_kernel(v_ref, right_ref, a_ref, older_ref, acc_ref):
    near_kernel(v_ref, right_ref, a_ref, acc_ref, older_ref)


def near_last_kernel(v_ref, right_ref, a_ref, acc_ref, copy_ref, sem):
    out = pltpu.make_async_copy(v_ref, copy_ref, sem)
    out.start()
    near_kernel(v_ref, right_ref, a_ref, acc_ref)
    out.wait()


def finish(acc_ref, left_ref, a_ref, new_ref, scale=1.0):
    rows = acc_ref.shape[1]
    step = 2 * B

    def run(halo, part):
        for i in range(0, rows, step):
            total = acc_ref[:, i : i + step] + scale * part(halo, a_ref, i, step)
            new_ref[:, i : i + step] = total.astype(new_ref.dtype)

    low, high = halo_sides(left_ref)
    pl.when(on_even_chip())(lambda: run(low, low_part))
    pl.when(jnp.logical_not(on_even_chip()))(lambda: run(high, high_part))


def on_first_core():
    return lax.axis_index("band") == 0


def on_even_chip():
    return lax.axis_index("z") % 2 == 0


def depart(new_ref, to_right_ref, to_left_ref):
    reach = DIST * B
    top = new_ref[:, new_ref.shape[1] - reach :]
    bottom = new_ref[:, :reach]
    to_right_ref[...] = jnp.where(on_even_chip(), top, bottom)
    to_left_ref[...] = jnp.where(on_even_chip(), bottom, top)


def first_kernel(acc_ref, left_ref, a_ref, new_ref, to_right_ref, to_left_ref):
    finish(acc_ref, left_ref, a_ref, new_ref)
    depart(new_ref, to_right_ref, to_left_ref)


def next_kernel(acc_ref, left_ref, a_ref, new_ref, to_right_ref, to_left_ref):
    finish(acc_ref, left_ref, a_ref, new_ref, 2.0)
    depart(new_ref, to_right_ref, to_left_ref)


def image_kernel(acc_ref, left_ref, a_ref, new_ref):
    finish(acc_ref, left_ref, a_ref, new_ref)


def in_vmem(kernel, name, outs, *args, flops=0):
    specs = [pl.BlockSpec(memory_space=pltpu.VMEM)]
    return pl.pallas_call(
        kernel,
        out_shape=[pltpu.VMEM(s, d) for s, d in outs],
        in_specs=specs * len(args),
        out_specs=specs * len(outs),
        compiler_params=pltpu.CompilerParams(vmem_limit_bytes=16 * MIB),
        cost_estimate=pl.CostEstimate(flops=flops, bytes_accessed=0, transcendentals=0),
        name=name,
    )(*args)


def gram_kernel(own_ref, other_ref, image_ref, other_image_ref, out_ref):
    own = own_ref[...]
    half = own.shape[0]
    is_first = on_first_core()

    def both(mine, others):
        a, b = dot_nt(own, mine), dot_nt(own, others)
        return jnp.concatenate([jnp.where(is_first, a, b), jnp.where(is_first, b, a)], axis=1)

    out_ref[:half, :] = both(own, other_ref[...])
    out_ref[half:, :] = both(image_ref[...], other_image_ref[...])


def exchange(to_right, to_left):
    count = lax.axis_size(ROWS)
    every = (*ROWS, "band")
    pairs = [(i, i + 1) for i in range(0, count, 2)], [(i, i + 1) for i in range(1, count - 1, 2)]
    right, left = [
        [(2 * a + core, 2 * b + core) for core in (0, 1) for i, j in p for a, b in ((i, j), (j, i))]
        for p in pairs
    ]
    for end in (0, count - 1):
        left += [(2 * end, 2 * end + 1), (2 * end + 1, 2 * end)]
    return lax.ppermute(to_right, every, right), lax.ppermute(to_left, every, left)


def from_other_core(value):
    return lax.ppermute(value, "band", [(0, 1), (1, 0)])


def sum_over_rows(value):
    count = lax.axis_size(ROWS)
    for distances in ((7,), (1, 2, 3), (8, 16, 24), (32, 64, 96)):
        own = lax.reduce_precision(value, exponent_bits=8, mantissa_bits=7)
        sent = own.astype(jnp.bfloat16)
        others = [
            lax.ppermute(sent, ROWS, [(i, i ^ d) for i in range(count)]).astype(jnp.float32)
            for d in distances
        ]
        value = own + others[0]
        if len(others) == 3:
            value = value + (others[1] + others[2])
    return value


def body(hamiltonian, neighbours, counts, vectors):
    block_rows = hamiltonian.shape[0]
    rows, width = vectors.shape
    reach = DIST * B
    field = ((width, rows), jnp.bfloat16)
    halo = ((width, reach), jnp.bfloat16)
    part = ((width, rows), jnp.float32)
    near_flops = 3 * width * rows * rows

    def near(v, right, name, *older):
        kernel = near_next_kernel if older else near_kernel
        return in_vmem(kernel, name, [part], v, right, band, *older, flops=near_flops)[0]

    start = vectors.T
    right, left = exchange(start, start)
    band = build_band(neighbours, counts, hamiltonian)
    acc = near(start, right, "near1")
    level1, *edges = in_vmem(first_kernel, "level1", [field, halo, halo], acc, left, band)
    older, newer = start, level1
    for degree in range(2, 5):
        right, left = exchange(*edges)
        acc = near(newer, right, "near%d" % degree, older)
        latest, *edges = in_vmem(
            next_kernel, "level%d" % degree, [field, halo, halo], acc, left, band
        )
        older, newer = newer, latest
    right, left = exchange(*edges)
    acc, filtered = pl.pallas_call(
        near_last_kernel,
        out_shape=[pltpu.VMEM(*part), pltpu.HBM(*field)],
        in_specs=[pl.BlockSpec(memory_space=pltpu.VMEM)] * 3,
        out_specs=[pl.BlockSpec(memory_space=pltpu.VMEM), pl.BlockSpec(memory_space=pltpu.HBM)],
        scratch_shapes=[pltpu.SemaphoreType.DMA],
        compiler_params=pltpu.CompilerParams(vmem_limit_bytes=16 * MIB),
        cost_estimate=pl.CostEstimate(flops=near_flops, bytes_accessed=0, transcendentals=0),
        name="near5",
    )(newer, right, band)
    acc, mine = lax.optimization_barrier((acc, newer))
    other = from_other_core(mine)
    (image,) = in_vmem(image_kernel, "image", [field], acc, left, band)
    other_image = from_other_core(image)
    sums = pl.pallas_call(
        gram_kernel,
        out_shape=jax.ShapeDtypeStruct((2 * width, 2 * width), jnp.float32),
        in_specs=[pl.BlockSpec(memory_space=pltpu.VMEM)] * 4,
        out_specs=pl.BlockSpec(memory_space=pltpu.VMEM),
        compiler_params=pltpu.CompilerParams(vmem_limit_bytes=16 * MIB),
        name="gram",
    )(newer, other, image, other_image)
    sums = sum_over_rows(sums) * (1.0 / (rows * lax.axis_size(ROWS)))
    return filtered.T, sums[:width], sums[width:]


def solution(mesh):
    shape = tuple(mesh.shape[name] for name in mesh.axis_names)
    chips = Mesh(mesh.devices.reshape(4, 4, 8, shape[1]), (*ROWS, "band"))
    return jax.shard_map(
        body,
        mesh=chips,
        in_specs=(P(ROWS, None, None, None), P(ROWS, None), P(ROWS), P(ROWS, "band")),
        out_specs=(P(ROWS, "band"), P("band", None), P("band", None)),
        check_vma=False,
    )
```
